32 devices in a mesh: seq: 8 (over z, y), tp: 4 (over x, core).
Axes of the slice: x: 2, y: 2, z: 4, core: 2. Of those that a mesh axis runs over, the one named last changes fastest.
Arguments:
- tier_source_concatenated: bfloat16 [1024, 2048], P('seq', 'tp'), may hold values from -6 to 6
- prompt_sizes_ordered: int32 [4], replicated, may hold values from 1 to 512, 1024 in all
- tier_standardize_scale: float32 [2048], replicated, may hold values from 0.1 to 1.9
- tier_standardize_offset: float32 [2048], replicated, may hold values from -3 to 3
- previous_item_mixers: float32 [5, 2048], replicated, may hold values from 0 to 1
- mapping_matrices_pile: bfloat16 [4, 2048, 2048], P(None, None, 'tp'), may hold values from -0.125 to 0.125
- fading_narrow_left: bfloat16 [2048, 64], replicated, may hold values from -0.125 to 0.125
- fading_narrow_right: bfloat16 [64, 2048], P(None, 'tp'), may hold values from -0.75 to 0.75
- feature_fading_baseline: float32 [2048], P('tp'), may hold values from 5e-05 to 0.04
- diagonal_boost_coefficient: float32 [2048], P('tp'), may hold values from -4 to 4
- cluster_standardize_scale: float32 [2048], P('tp'), may hold values from 0.1 to 1.9
- cluster_standardize_offset: float32 [2048], P('tp'), may hold values from -3 to 3
- emitted_mapping_matrix: bfloat16 [2048, 2048], P('tp'), may hold values from -0.125 to 0.125
Outputs:
- hidden_out: bfloat16 [1024, 2048], P('seq', 'tp')
The draws below stay inside these ranges and needn't reach their ends.
Inputs may be any that keep to these rules, and one draw needn't show every extreme that they name: `prompt_sizes_ordered`: the prompt lengths sum to 1024, and the longest is exactly 512.
All inputs are finite; a program needn't handle non-finite values.
Results may differ from the reference program's by a relative error of at most 0.025.
Values may be sent and summed in bfloat16 or wider, within the bound.
A program may use at most 128 MiB of HBM per device.

```python
import math
import jax
import jax.numpy as jnp
import numpy as np
from jax import lax

EMBEDDING_SIZE = 2048
CHANNELS_ONE_HEAD = 64
DL = 64
TOKENS = 1024
REQUESTS = 4
MAX_LEN = 512


def steps_of(stream_key, extent, shards, smallest, high):
    level = 1.0
    for axis_at, blocks in shards:
        steps = jax.random.uniform(jax.random.fold_in(jax.random.fold_in(stream_key, 6), axis_at), (blocks,), jnp.float32, smallest / len(shards), high / len(shards))
        level = level * jnp.repeat(jnp.exp(steps), extent[axis_at] // blocks).reshape((-1,) + (1,) * (len(extent) - 1 - axis_at))
    return level


def profile(count, total, limit, skew):
    weights = [(1 << 20) // math.isqrt(standing ** skew) + 1 for standing in range(2, count + 1)]
    rest, holding = total - limit - (count - 1), [1] * (count - 1)
    while rest > 0:
        candidates = [i for i in range(count - 1) if holding[i] < limit]
        mass, remaining = sum([weights[i] for i in candidates]), rest
        for i in candidates:
            addition = min(limit - holding[i], max(1, remaining * weights[i] // mass), rest)
            holding[i] = holding[i] + addition
            rest = rest - addition
    return np.array([limit] + holding)


def uneven_parts(own_key, count, total, bound, slope):
    if count == 2:
        one = jax.random.randint(own_key, (), max(1, total - bound), min(bound, total - 1) + 1)
        return jnp.stack([one, total - one])
    tallies = jnp.asarray(profile(count, total, bound, slope), jnp.int32)
    pairs = (count - 1) // 2
    source_of, taker = tallies[1:1 + 2 * pairs:2], tallies[2:2 + 2 * pairs:2]
    margin = jnp.minimum(source_of - 1, bound - taker)
    shifted = jax.random.randint(jax.random.fold_in(own_key, 1), (pairs,), 0, 1 << 20) % (margin + 1)
    tallies = tallies.at[1:1 + 2 * pairs:2].set(source_of - shifted).at[2:2 + 2 * pairs:2].set(taker + shifted)
    return tallies[jax.random.permutation(jax.random.fold_in(own_key, 2), count)]


def normal_values(stream_key, extent, deviation, most, split=(), kind=jnp.bfloat16):
    level = steps_of(stream_key, extent, split, -0.22, 0.18) if split else 1.0
    result = jax.random.normal(stream_key, extent, jnp.float32) * deviation * level
    return jnp.minimum(jnp.maximum(result, -most), most).astype(kind)


def setup_inputs(seed: int = 0) -> dict:
    streams_of = jax.random.split(jax.random.key(seed), 14)
    tier_source_concatenated = normal_values(streams_of[0], (TOKENS, EMBEDDING_SIZE), 1.0, 6.0, ((0, 8), (1, 4)))
    prompt_sizes_ordered = uneven_parts(streams_of[1], REQUESTS, TOKENS, MAX_LEN, 2).astype(jnp.int32)
    tier_standardize_scale = jnp.clip(1.0 + 0.18 * jax.random.normal(streams_of[2], (EMBEDDING_SIZE,), jnp.float32), 0.1, 1.9)
    tier_standardize_offset = normal_values(streams_of[3], (EMBEDDING_SIZE,), 0.5, 3.0, (), jnp.float32)
    previous_item_mixers = jnp.clip(jax.random.uniform(streams_of[4], (5, EMBEDDING_SIZE), jnp.float32, 0.0, 1.0), 0.0, 1.0)
    mapping_matrices_pile = normal_values(streams_of[5], (4, EMBEDDING_SIZE, EMBEDDING_SIZE), EMBEDDING_SIZE ** -0.5, 0.125, ((2, 4),))
    fading_narrow_left = normal_values(streams_of[6], (EMBEDDING_SIZE, DL), EMBEDDING_SIZE ** -0.5, 0.125)
    fading_narrow_right = normal_values(streams_of[7], (DL, EMBEDDING_SIZE), DL ** -0.5, 0.75, ((1, 4),))
    feature_fading_baseline = jnp.clip(jnp.exp(math.log(0.04) - 6.684612 * jax.random.uniform(streams_of[8], (EMBEDDING_SIZE,), jnp.float32) ** steps_of(streams_of[8], (EMBEDDING_SIZE,), ((0, 4),), -0.2, 0.2)), 4.999999873689376e-05, 0.04)
    diagonal_boost_coefficient = normal_values(streams_of[9], (EMBEDDING_SIZE,), 1.0, 4.0, ((0, 4),), jnp.float32)
    cluster_standardize_scale = jnp.clip(1.0 + 0.18 * jax.random.normal(streams_of[10], (EMBEDDING_SIZE,), jnp.float32), 0.1, 1.9)
    cluster_standardize_offset = normal_values(streams_of[11], (EMBEDDING_SIZE,), 0.5, 3.0, ((0, 4),), jnp.float32)
    emitted_mapping_matrix = normal_values(streams_of[12], (EMBEDDING_SIZE, EMBEDDING_SIZE), EMBEDDING_SIZE ** -0.5, 0.125, ((0, 4),))
    return {"tier_source_concatenated": tier_source_concatenated, "prompt_sizes_ordered": prompt_sizes_ordered, "tier_standardize_scale": tier_standardize_scale, "tier_standardize_offset": tier_standardize_offset, "previous_item_mixers": previous_item_mixers, "mapping_matrices_pile": mapping_matrices_pile, "fading_narrow_left": fading_narrow_left, "fading_narrow_right": fading_narrow_right, "feature_fading_baseline": feature_fading_baseline, "diagonal_boost_coefficient": diagonal_boost_coefficient, "cluster_standardize_scale": cluster_standardize_scale, "cluster_standardize_offset": cluster_standardize_offset, "emitted_mapping_matrix": emitted_mapping_matrix}


def layer_norm(rows, gain, bias, eps):
    mean = lax.optimization_barrier(jnp.mean(rows, axis=-1, keepdims=True))
    centred = rows - mean
    spread = lax.optimization_barrier(jnp.mean(centred * centred, axis=-1, keepdims=True))
    return centred * lax.rsqrt(spread + eps) * gain + bias

def reference(tier_source_concatenated, prompt_sizes_ordered, tier_standardize_scale, tier_standardize_offset, previous_item_mixers, mapping_matrices_pile, fading_narrow_left, fading_narrow_right, feature_fading_baseline, diagonal_boost_coefficient, cluster_standardize_scale, cluster_standardize_offset, emitted_mapping_matrix):
    total = tier_source_concatenated.shape[0]
    width = tier_source_concatenated.shape[1]
    mixing_values_divided = width // CHANNELS_ONE_HEAD
    first = (jnp.cumsum(prompt_sizes_ordered) - prompt_sizes_ordered).astype(jnp.int32)
    position = jnp.arange(total, dtype=jnp.int32)
    is_start = jnp.any(position[:, None] == first[None, :], axis=1)
    normed = layer_norm(tier_source_concatenated.astype(jnp.float32), tier_standardize_scale, tier_standardize_offset, 1e-05).astype(jnp.bfloat16)
    previous = jnp.concatenate([jnp.zeros((1, width), jnp.bfloat16), normed[:-1]], axis=0)
    previous = jnp.where(is_start[:, None], jnp.zeros_like(previous), previous)
    base = normed.astype(jnp.float32)
    delta = previous.astype(jnp.float32) - base
    outputs = []
    for index in range(4):
        shifted_blend = (base + delta * previous_item_mixers[index][None, :]).astype(jnp.bfloat16)
        outputs.append(jnp.dot(shifted_blend, mapping_matrices_pile[index], preferred_element_type=jnp.float32))
    recept = outputs[0].astype(jnp.bfloat16)
    key_rows = outputs[1].astype(jnp.bfloat16)
    value_rows = outputs[2].astype(jnp.bfloat16)
    gate = jax.nn.silu(outputs[3]).astype(jnp.bfloat16)
    decay_shifted_blend = (base + delta * previous_item_mixers[4][None, :]).astype(jnp.bfloat16)
    lowrank_decay_delta = jnp.tanh(jnp.dot(decay_shifted_blend, fading_narrow_left, preferred_element_type=jnp.float32)).astype(jnp.bfloat16)
    decay_logarithm = -feature_fading_baseline[None, :] * jnp.exp(jnp.dot(lowrank_decay_delta, fading_narrow_right, preferred_element_type=jnp.float32))
    r_all = recept.astype(jnp.float32).reshape(total, mixing_values_divided, CHANNELS_ONE_HEAD)
    k_all = key_rows.astype(jnp.float32).reshape(total, mixing_values_divided, CHANNELS_ONE_HEAD)
    v_all = value_rows.astype(jnp.float32).reshape(total, mixing_values_divided, CHANNELS_ONE_HEAD)
    d_all = jnp.exp(decay_logarithm).reshape(total, mixing_values_divided, CHANNELS_ONE_HEAD)
    diagonal_extra_contribution = diagonal_boost_coefficient.reshape(mixing_values_divided, CHANNELS_ONE_HEAD)

    def step(running_recurrence_array, item):
        gating_vector_here, k_t, v_t, d_t, s_t = item
        running_recurrence_array = jnp.where(s_t, jnp.zeros_like(running_recurrence_array), running_recurrence_array)
        query_vector_product = k_t[:, :, None] * v_t[:, None, :]
        level_ultimate_outcome = jnp.einsum('yr,yrk->yk', gating_vector_here, running_recurrence_array + diagonal_extra_contribution[:, :, None] * query_vector_product, precision=lax.Precision.HIGHEST)
        running_recurrence_array = d_t[:, :, None] * running_recurrence_array + query_vector_product
        return (running_recurrence_array, level_ultimate_outcome)
    init = jnp.zeros((mixing_values_divided, CHANNELS_ONE_HEAD, CHANNELS_ONE_HEAD), jnp.float32)
    _, wkv = lax.scan(step, init, (r_all, k_all, v_all, d_all, is_start))
    mean = lax.optimization_barrier(jnp.mean(wkv, axis=-1, keepdims=True))
    centred = wkv - mean
    spread = lax.optimization_barrier(jnp.mean(centred * centred, axis=-1, keepdims=True))
    grouped = (centred * lax.rsqrt(spread + 0.00064)).reshape(total, width) * cluster_standardize_scale + cluster_standardize_offset
    gated = (grouped * gate.astype(jnp.float32)).astype(jnp.bfloat16)
    projected = jnp.dot(gated, emitted_mapping_matrix, preferred_element_type=jnp.float32)
    return (tier_source_concatenated.astype(jnp.float32) + projected).astype(jnp.bfloat16)
```

```python
import functools

import jax
import jax.numpy as jnp
import numpy as np
from jax import lax
from jax.experimental import pallas as pl
from jax.experimental.pallas import tpu as pltpu
from jax.sharding import PartitionSpec as P

HEAD = 64
GROUP = 256
EDGE = 16
BF16, F32 = jnp.bfloat16, jnp.float32
NT = (((1,), (1,)), ((), ()))
TN = (((0,), (0,)), ((), ()))


def span_matrix(rows):
    t, j = np.arange(rows)[:, None], np.arange(rows)[None, :]
    parts = []
    for level in range(rows.bit_length() - 1):
        same = (t >> level) == (j >> level)
        odd = ((t >> level) & 1) == 1
        parts.append(same & np.where(odd, j < t, j > t))
    parts += [j < t, j > t, np.ones((16, rows), bool)]
    spans = np.concatenate(parts, 0)
    return np.concatenate([spans, spans], 1).astype(jnp.bfloat16)


def dot(a, b, dims=None):
    if dims is None:
        return jnp.dot(a, b, preferred_element_type=F32)
    return lax.dot_general(a, b, dims, preferred_element_type=F32)


def kernel(
    n, sizes, x, gain, bias, mixers, fading, boost, head_gain, head_bias,
    spans_h, left_h, right_h, pile_h, emitted_h, out,
    xall, edge, spans, left, right, pile, emitted, mixed, rkvg, gated,
    mine, near, far, wide, came, give_far, got_far, give_near, got_near, give_sum, got_sum,
    load_sem, send_sem, recv_sem,
):
    rows, width = x.shape
    levels = rows.bit_length() - 1
    features = 4 * width
    groups = width // GROUP
    per_group = GROUP // HEAD
    s, t = lax.axis_index("seq"), lax.axis_index("tp")
    mate = t + 1 - 2 * lax.rem(t, 2)
    across = t + 2 - 4 * lax.div(t, 2)
    corner = 3 - t

    def ahead(d):
        return lax.rem(s + d, n)

    def behind(d):
        return lax.rem(s + n - d, n)

    loads = [
        (left_h, left), (spans_h, spans), (right_h, right),
        (pile_h.at[1], pile.at[1]), (pile_h.at[2], pile.at[2]),
        (pile_h.at[0], pile.at[0]), (pile_h.at[3], pile.at[3]), (emitted_h, emitted),
    ]
    loads = [pltpu.make_async_copy(a, b, load_sem.at[i]) for i, (a, b) in enumerate(loads)]
    left_in, spans_in, right_in, key_in, value_in, recept_in, gate_in, emitted_in = loads
    for load in loads:
        load.start()

    hops = [1, 2]
    while hops[-1] * 2 < n // 2:
        hops.append(hops[-1] * 2)
    doublings = [d for d in hops if 2 <= d < n // 2]

    barrier = pltpu.get_barrier_semaphore()
    sources = [(s, mate), (s, across)] + [(behind(1), jnp.int32(j)) for j in range(4)]
    sources += [(behind(d), t) for d in hops[1:]]
    for source in sources:
        pl.semaphore_signal(barrier, inc=1, device_id=source, device_id_type=pl.DeviceIdType.MESH)
    pl.semaphore_wait(barrier, len(sources))

    def remote(src, dst, index, device):
        return pltpu.make_async_remote_copy(
            src_ref=src, dst_ref=dst, send_sem=send_sem.at[index], recv_sem=recv_sem.at[index],
            device_id=device, device_id_type=pl.DeviceIdType.MESH,
        )

    over = remote(x, xall.at[t], 0, (s, across))
    over.start()
    side = remote(x, xall.at[t], 1, (s, mate))
    side.start()
    tail_rows = x.at[pl.ds(rows - EDGE, EDGE)]
    edges = [
        remote(tail_rows, edge.at[t], 2 + j, (ahead(1), lax.rem(t + j, 4))) for j in range(4)
    ]
    for copy in edges:
        copy.start()
    xall[t] = x[...]

    firsts = [jnp.int32(0)]
    for i in range(sizes.shape[0] - 1):
        firsts.append(firsts[-1] + sizes[i])

    def prompt_of(position):
        count = jnp.where(firsts[0] <= position, 1, 0)
        for first in firsts[1:]:
            count = count + jnp.where(first <= position, 1, 0)
        return count

    begin = s * rows
    order = lax.broadcasted_iota(jnp.int32, (rows, 1), 0)
    starts = begin + order == firsts[0]
    for first in firsts[1:]:
        starts = starts | (begin + order == first)
    going = jnp.where(starts, 0.0, 1.0)
    prompt = prompt_of(begin + order)
    entering, last = prompt_of(begin - 1), prompt_of(begin + rows - 1)
    valid = jnp.where(prompt == entering, 1.0, 0.0)
    tail_ok = jnp.where(prompt == last, 1.0, 0.0)
    keep = jnp.where(last == entering, 1.0, 0.0)

    over.wait_recv()
    pass_on = remote(xall.at[across], xall.at[across], 6, (s, mate))
    pass_on.start()
    side.wait_recv()
    for copy in edges:
        copy.wait_recv()
    pass_on.wait_recv()

    def moments(ref):
        total = sum(jnp.sum(ref[c].astype(F32), axis=1, keepdims=True) for c in range(4))
        mean = total / features
        square = 0.0
        for c in range(4):
            centred = ref[c].astype(F32) - mean
            square = square + jnp.sum(centred * centred, axis=1, keepdims=True)
        return mean, lax.rsqrt(square / features + 1e-5)

    mean, scale = moments(xall)
    edge_mean, edge_scale = moments(edge)
    for c in range(4):
        cols = slice(c * width, (c + 1) * width)
        base = ((xall[c].astype(F32) - mean) * scale * gain[:, cols] + bias[:, cols])
        base = base.astype(BF16).astype(F32)
        end = ((edge[c].astype(F32) - edge_mean) * edge_scale * gain[:, cols] + bias[:, cols])
        end = end.astype(BF16).astype(F32)
        previous = jnp.where(order == 0, end[EDGE - 1 :, :], pltpu.roll(base, 1, 0)) * going
        delta = previous - base
        for i in range(5):
            mixed[i, :, cols] = (base + delta * mixers[i : i + 1, cols]).astype(BF16)

    left_in.wait()
    right_in.wait()
    lora = jnp.tanh(dot(mixed[4], left[...])).astype(BF16)
    log_decay = -fading[...] * jnp.exp(dot(lora, right[...]))
    high = log_decay.astype(BF16)
    low = (log_decay - high.astype(F32)).astype(BF16)
    pair = jnp.concatenate([high, low], axis=0)
    spans_in.wait()

    def decays(block, lanes, count=rows):
        return jnp.exp(dot(spans[pl.ds(block * rows, count)], pair[:, lanes]))

    key_in.wait()
    rkvg[1] = dot(mixed[1], pile[1]).astype(BF16)
    value_in.wait()
    rkvg[2] = dot(mixed[2], pile[2]).astype(BF16)

    lane = lax.broadcasted_iota(jnp.int32, (1, GROUP), 1)
    of_head = [lane // HEAD == h for h in range(per_group)]
    ones_of = [jnp.where(m, 1.0, 0.0).astype(BF16) for m in of_head]
    all_lanes = [slice(g * GROUP, (g + 1) * GROUP) for g in range(groups)]
    for lanes in all_lanes:
        tail = (rkvg[1, :, lanes].astype(F32) * decays(levels + 1, lanes) * tail_ok).astype(BF16)
        full = dot(rkvg[2, :, lanes], tail, TN)
        state = jnp.where(of_head[0], full[:HEAD], 0.0)
        for h in range(1, per_group):
            state = state + jnp.where(of_head[h], full[h * HEAD : (h + 1) * HEAD], 0.0)
        mine[:HEAD, lanes] = state.astype(BF16)
        mine[HEAD:, lanes] = (decays(levels + 2, lanes, 16) * keep).astype(BF16)
    to_near = remote(mine, near, 7, (ahead(1), t))
    to_near.start()
    to_far = remote(mine, far, 8, (ahead(2), t))
    to_far.start()

    recept_in.wait()
    rkvg[0] = dot(mixed[0], pile[0]).astype(BF16)

    row = lax.broadcasted_iota(jnp.int32, (rows, rows), 0)
    col = lax.broadcasted_iota(jnp.int32, (rows, rows), 1)
    together = prompt_of(begin + row) == prompt_of(begin + col)

    def pair_mask(level):
        if level == levels:
            return jnp.where(row == col, 1.0, 0.0)
        ok = (row >> (level + 1)) == (col >> (level + 1))
        ok = ok & (((row >> level) & 1) == 1) & (((col >> level) & 1) == 0)
        return jnp.where(ok & together, 1.0, 0.0)

    def local_part(lanes):
        recept, key, value = rkvg[0, :, lanes], rkvg[1, :, lanes], rkvg[2, :, lanes]
        scores = [0.0] * per_group
        for level in range(levels + 1):
            if level < levels:
                weight = decays(level, lanes).astype(BF16)
                asks, keys = recept * weight, key * weight
            else:
                asks, keys = (recept.astype(F32) * boost[:, lanes]).astype(BF16), key
            asks = jnp.concatenate([asks * m for m in ones_of], axis=0)
            found = dot(asks, keys, NT)
            mask = pair_mask(level)
            scores = [
                scores[h] + found[h * rows : (h + 1) * rows] * mask for h in range(per_group)
            ]
        scores = jnp.concatenate([p.astype(BF16) for p in scores], axis=1)
        values = jnp.concatenate([value * m for m in ones_of], axis=0)
        return dot(scores, values)

    local = [local_part(all_lanes[0])]

    to_near.wait_recv()
    to_far.wait_recv()
    reach = near[HEAD:].astype(F32)[:1]
    state = near[:HEAD].astype(F32) + reach * far[:HEAD].astype(F32)
    reach = reach * far[HEAD:].astype(F32)[:1]
    sent = []
    for i, d in enumerate(doublings):
        wide[i, :HEAD] = state.astype(BF16)
        wide[i, HEAD:] = jnp.broadcast_to(reach, (16, width)).astype(BF16)
        copy = remote(wide.at[i], came.at[i], 9 + i, (ahead(d), t))
        copy.start()
        sent.append(copy)
        if i == 0:
            local += [local_part(lanes) for lanes in all_lanes[1:]]
            gate_in.wait()
            gate = dot(mixed[3], pile[3])
            rkvg[3] = (gate / (1.0 + jnp.exp(-gate))).astype(BF16)
        copy.wait_recv()
        state = state + reach * came[i, :HEAD].astype(F32)
        reach = reach * came[i, HEAD:].astype(F32)[:1]

    r2 = lax.broadcasted_iota(jnp.int32, (2 * GROUP, GROUP), 0)
    c2 = lax.broadcasted_iota(jnp.int32, (2 * GROUP, GROUP), 1)
    averager = jnp.where(lax.rem(r2, GROUP) // HEAD == c2 // HEAD, 1.0 / HEAD, 0.0).astype(BF16)
    for g, lanes in enumerate(all_lanes):
        carried = (rkvg[0, :, lanes].astype(F32) * decays(levels, lanes) * valid).astype(BF16)
        held = state[:, lanes].astype(BF16)
        held = jnp.concatenate([held * m for m in ones_of], axis=0)
        wkv = local[g] + dot(carried, held, NT)
        big = wkv.astype(BF16)
        small = (wkv - big.astype(F32)).astype(BF16)
        centred = wkv - dot(jnp.concatenate([big, small], axis=1), averager)
        spread = dot((centred * centred).astype(BF16), averager[:GROUP])
        grouped = centred * lax.rsqrt(spread + 6.4e-4) * head_gain[:, lanes] + head_bias[:, lanes]
        gated[:, lanes] = (grouped * rkvg[3, :, lanes].astype(F32)).astype(BF16)

    emitted_in.wait()

    def partial(block):
        return dot(gated[...], emitted[:, pl.ds(pl.multiple_of(block * width, width), width)])

    index = 9 + len(doublings)
    give_far[...] = partial(corner).astype(BF16)
    first_give = remote(give_far, got_far, index, (s, mate))
    first_give.start()
    for_across = partial(across)
    first_give.wait_recv()
    give_sum[...] = (for_across + got_far[...].astype(F32)).astype(BF16)
    sum_give = remote(give_sum, got_sum, index + 1, (s, across))
    sum_give.start()
    give_near[...] = partial(mate).astype(BF16)
    second_give = remote(give_near, got_near, index + 2, (s, mate))
    second_give.start()
    total = x[...].astype(F32) + partial(t)
    second_give.wait_recv()
    total = total + got_near[...].astype(F32)
    sum_give.wait_recv()
    out[...] = (total + got_sum[...].astype(F32)).astype(BF16)

    for copy in [over, side, *edges, pass_on, to_near, to_far, *sent]:
        copy.wait_send()
    for copy in [first_give, sum_give, second_give]:
        copy.wait_send()


def body(n, x, sizes, gain, bias, mixers, pile, left, right, fading, boost, head_gain, head_bias, emitted):
    rows, width = x.shape
    features, rank = left.shape
    doublings = max(1, (n // 2).bit_length() - 2)
    copies = 9 + doublings + 3
    spans = span_matrix(rows)
    vmem, anywhere = pl.BlockSpec(memory_space=pltpu.VMEM), pl.BlockSpec(memory_space=pl.ANY)
    message = pltpu.VMEM((HEAD + 16, width), BF16)
    messages = pltpu.VMEM((doublings, HEAD + 16, width), BF16)
    block = pltpu.VMEM((rows, width), BF16)
    return pl.pallas_call(
        functools.partial(kernel, n),
        out_shape=jax.ShapeDtypeStruct((rows, width), BF16),
        in_specs=[pl.BlockSpec(memory_space=pltpu.SMEM)] + [vmem] * 8 + [anywhere] * 5,
        out_specs=vmem,
        scratch_shapes=[
            pltpu.VMEM((4, rows, width), BF16),
            pltpu.VMEM((4, EDGE, width), BF16),
            pltpu.VMEM(spans.shape, BF16),
            pltpu.VMEM((features, rank), BF16),
            pltpu.VMEM((rank, width), BF16),
            pltpu.VMEM(pile.shape, BF16),
            pltpu.VMEM(emitted.shape, BF16),
            pltpu.VMEM((5, rows, features), BF16),
            pltpu.VMEM((4, rows, width), BF16),
            block,
            message, message, message, messages, messages,
            block, block, block, block, block, block,
            pltpu.SemaphoreType.DMA((8,)),
            pltpu.SemaphoreType.DMA((copies,)),
            pltpu.SemaphoreType.DMA((copies,)),
        ],
        compiler_params=pltpu.CompilerParams(
            collective_id=0, has_side_effects=True, vmem_limit_bytes=48 * 1024 * 1024
        ),
    )(
        sizes, x, gain[None], bias[None], mixers, fading[None], boost[None],
        head_gain[None], head_bias[None], jnp.asarray(spans), left, right, pile, emitted,
    )


def solution(mesh):
    in_specs = (
        P("seq", "tp"), P(), P(), P(), P(), P(None, None, "tp"), P(), P(None, "tp"),
        P("tp"), P("tp"), P("tp"), P("tp"), P("tp", None),
    )
    return jax.shard_map(
        functools.partial(body, mesh.shape["seq"]),
        mesh=mesh, in_specs=in_specs, out_specs=P("seq", "tp"), check_vma=False,
    )
```

```python
import functools

import jax
import jax.numpy as jnp
import numpy as np
from jax import lax
from jax.experimental import pallas as pl
from jax.experimental.pallas import tpu as pltpu
from jax.sharding import PartitionSpec as P

HEAD = 64
GROUP = 256
EDGE = 16
BF16, F32 = jnp.bfloat16, jnp.float32
NT = (((1,), (1,)), ((), ()))
TN = (((0,), (0,)), ((), ()))


def span_matrix(rows):
    t, j = np.arange(rows)[:, None], np.arange(rows)[None, :]
    parts = []
    for level in range(rows.bit_length() - 1):
        same = (t >> level) == (j >> level)
        odd = ((t >> level) & 1) == 1
        parts.append(same & np.where(odd, j < t, j > t))
    parts += [j < t, j > t, np.ones((16, rows), bool)]
    spans = np.concatenate(parts, 0)
    return np.concatenate([spans, spans], 1).astype(jnp.bfloat16)


def dot(a, b, dims=None):
    if dims is None:
        return jnp.dot(a, b, preferred_element_type=F32)
    return lax.dot_general(a, b, dims, preferred_element_type=F32)


def kernel(
    n, sizes_h, x, gain_h, bias_h, mixers_h, fading_h, boost_h, head_gain_h, head_bias_h,
    spans_h, left_h, right_h, pile_h, emitted_h, out,
    sizes, gain, bias, mixers, fading, boost, head_gain, head_bias, xall, edge, spans, left, right, pile, emitted, mixed, rkvg, gated,
    mine, near, far, wide, came, give_far, got_far, give_near, got_near, give_sum, got_sum,
    load_sem, send_sem, recv_sem,
):
    rows, width = x.shape
    levels = rows.bit_length() - 1
    features = 4 * width
    groups = width // GROUP
    per_group = GROUP // HEAD
    s, t = lax.axis_index("seq"), lax.axis_index("tp")
    mate = t + 1 - 2 * lax.rem(t, 2)
    across = t + 2 - 4 * lax.div(t, 2)
    corner = 3 - t

    def ahead(d):
        return lax.rem(s + d, n)

    def behind(d):
        return lax.rem(s + n - d, n)

    wanted = [
        (x, xall.at[t]), (sizes_h, sizes), (gain_h, gain), (bias_h, bias), (mixers_h, mixers),
        (left_h, left), (right_h, right), (fading_h, fading), (spans_h, spans),
        (pile_h.at[1], pile.at[1]), (pile_h.at[2], pile.at[2]), (pile_h.at[0], pile.at[0]),
        (boost_h, boost), (pile_h.at[3], pile.at[3]), (head_gain_h, head_gain),
        (head_bias_h, head_bias), (emitted_h, emitted),
    ]
    loads = [pltpu.make_async_copy(a, b, load_sem.at[i]) for i, (a, b) in enumerate(wanted)]
    for load in loads:
        load.start()
    unread = list(loads)

    def ready(upto):
        while len(loads) - len(unread) < upto:
            unread.pop(0).wait()

    hops = [1, 2]
    while hops[-1] * 2 < n // 2:
        hops.append(hops[-1] * 2)
    doublings = [d for d in hops if 2 <= d < n // 2]

    barrier = pltpu.get_barrier_semaphore()
    sources = [(s, mate), (s, across)] + [(behind(1), jnp.int32(j)) for j in range(4)]
    sources += [(behind(d), t) for d in hops[1:]]
    for source in sources:
        pl.semaphore_signal(barrier, inc=1, device_id=source, device_id_type=pl.DeviceIdType.MESH)
    pl.semaphore_wait(barrier, len(sources))

    def remote(src, dst, index, device):
        return pltpu.make_async_remote_copy(
            src_ref=src, dst_ref=dst, send_sem=send_sem.at[index], recv_sem=recv_sem.at[index],
            device_id=device, device_id_type=pl.DeviceIdType.MESH,
        )

    over = remote(x, xall.at[t], 0, (s, across))
    over.start()
    side = remote(x, xall.at[t], 1, (s, mate))
    side.start()
    tail_rows = x.at[pl.ds(rows - EDGE, EDGE)]
    edges = [
        remote(tail_rows, edge.at[t], 2 + j, (ahead(1), lax.rem(t + j, 4))) for j in range(4)
    ]
    for copy in edges:
        copy.start()
    ready(2)

    firsts = [jnp.int32(0)]
    for i in range(sizes.shape[0] - 1):
        firsts.append(firsts[-1] + sizes[i])

    def prompt_of(position):
        count = jnp.where(firsts[0] <= position, 1, 0)
        for first in firsts[1:]:
            count = count + jnp.where(first <= position, 1, 0)
        return count

    begin = s * rows
    order = lax.broadcasted_iota(jnp.int32, (rows, 1), 0)
    starts = begin + order == firsts[0]
    for first in firsts[1:]:
        starts = starts | (begin + order == first)
    going = jnp.where(starts, 0.0, 1.0)
    prompt = prompt_of(begin + order)
    entering, last = prompt_of(begin - 1), prompt_of(begin + rows - 1)
    valid = jnp.where(prompt == entering, 1.0, 0.0)
    tail_ok = jnp.where(prompt == last, 1.0, 0.0)
    keep = jnp.where(last == entering, 1.0, 0.0)

    over.wait_recv()
    pass_on = remote(xall.at[across], xall.at[across], 6, (s, mate))
    pass_on.start()
    side.wait_recv()
    for copy in edges:
        copy.wait_recv()
    pass_on.wait_recv()


    ready(5)

    def moments(ref):
        total = sum(jnp.sum(ref[c].astype(F32), axis=1, keepdims=True) for c in range(4))
        mean = total / features
        square = 0.0
        for c in range(4):
            centred = ref[c].astype(F32) - mean
            square = square + jnp.sum(centred * centred, axis=1, keepdims=True)
        return mean, lax.rsqrt(square / features + 1e-5)

    mean, scale = moments(xall)
    edge_mean, edge_scale = moments(edge)
    for c in range(4):
        cols = slice(c * width, (c + 1) * width)
        base = ((xall[c].astype(F32) - mean) * scale * gain[:, cols] + bias[:, cols])
        base = base.astype(BF16).astype(F32)
        end = ((edge[c].astype(F32) - edge_mean) * edge_scale * gain[:, cols] + bias[:, cols])
        end = end.astype(BF16).astype(F32)
        previous = jnp.where(order == 0, end[EDGE - 1 :, :], pltpu.roll(base, 1, 0)) * going
        delta = previous - base
        for i in range(5):
            mixed[i, :, cols] = (base + delta * mixers[i : i + 1, cols]).astype(BF16)


    ready(9)
    lora = jnp.tanh(dot(mixed[4], left[...], NT)).astype(BF16)
    log_decay = -fading[...] * jnp.exp(dot(lora, right[...]))
    high = log_decay.astype(BF16)
    low = (log_decay - high.astype(F32)).astype(BF16)
    pair = jnp.concatenate([high, low], axis=0)

    def decays(block, lanes, count=rows):
        return jnp.exp(dot(spans[pl.ds(block * rows, count)], pair[:, lanes]))


    ready(10)
    rkvg[1] = dot(mixed[1], pile[1]).astype(BF16)
    ready(11)
    rkvg[2] = dot(mixed[2], pile[2]).astype(BF16)


    lane = lax.broadcasted_iota(jnp.int32, (1, GROUP), 1)
    of_head = [lane // HEAD == h for h in range(per_group)]
    ones_of = [jnp.where(m, 1.0, 0.0).astype(BF16) for m in of_head]
    all_lanes = [slice(g * GROUP, (g + 1) * GROUP) for g in range(groups)]
    for lanes in all_lanes:
        tail = (rkvg[1, :, lanes].astype(F32) * decays(levels + 1, lanes) * tail_ok).astype(BF16)
        full = dot(rkvg[2, :, lanes], tail, TN)
        state = jnp.where(of_head[0], full[:HEAD], 0.0)
        for h in range(1, per_group):
            state = state + jnp.where(of_head[h], full[h * HEAD : (h + 1) * HEAD], 0.0)
        mine[:HEAD, lanes] = state.astype(BF16)
        mine[HEAD:, lanes] = (decays(levels + 2, lanes, 16) * keep).astype(BF16)
    to_near = remote(mine, near, 7, (ahead(1), t))
    to_near.start()
    to_far = remote(mine, far, 8, (ahead(2), t))
    to_far.start()


    ready(13)
    rkvg[0] = dot(mixed[0], pile[0]).astype(BF16)


    row = lax.broadcasted_iota(jnp.int32, (rows, rows), 0)
    col = lax.broadcasted_iota(jnp.int32, (rows, rows), 1)
    together = prompt_of(begin + row) == prompt_of(begin + col)

    def pair_mask(level):
        if level == levels:
            return jnp.where(row == col, 1.0, 0.0)
        ok = (row >> (level + 1)) == (col >> (level + 1))
        ok = ok & (((row >> level) & 1) == 1) & (((col >> level) & 1) == 0)
        return jnp.where(ok & together, 1.0, 0.0)

    def local_part(lanes):
        recept, key, value = rkvg[0, :, lanes], rkvg[1, :, lanes], rkvg[2, :, lanes]
        scores = [0.0] * per_group
        for level in range(levels + 1):
            if level < levels:
                weight = decays(level, lanes).astype(BF16)
                asks, keys = recept * weight, key * weight
            else:
                asks, keys = (recept.astype(F32) * boost[:, lanes]).astype(BF16), key
            asks = jnp.concatenate([asks * m for m in ones_of], axis=0)
            found = dot(asks, keys, NT)
            mask = pair_mask(level)
            scores = [
                scores[h] + found[h * rows : (h + 1) * rows] * mask for h in range(per_group)
            ]
        scores = jnp.concatenate([p.astype(BF16) for p in scores], axis=1)
        values = jnp.concatenate([value * m for m in ones_of], axis=0)
        return dot(scores, values)

    local = [local_part(all_lanes[0])]


    to_near.wait_recv()
    to_far.wait_recv()

    reach = near[HEAD:].astype(F32)[:1]
    state = near[:HEAD].astype(F32) + reach * far[:HEAD].astype(F32)
    reach = reach * far[HEAD:].astype(F32)[:1]
    sent = []
    for i, d in enumerate(doublings):
        wide[i, :HEAD] = state.astype(BF16)
        wide[i, HEAD:] = jnp.broadcast_to(reach, (16, width)).astype(BF16)
        copy = remote(wide.at[i], came.at[i], 9 + i, (ahead(d), t))
        copy.start()
        sent.append(copy)
        if i == 0:
            local += [local_part(lanes) for lanes in all_lanes[1:]]
            ready(14)
            gate = dot(mixed[3], pile[3])
            rkvg[3] = (gate / (1.0 + jnp.exp(-gate))).astype(BF16)
        copy.wait_recv()
        state = state + reach * came[i, :HEAD].astype(F32)
        reach = reach * came[i, HEAD:].astype(F32)[:1]


    ready(16)
    r2 = lax.broadcasted_iota(jnp.int32, (2 * GROUP, GROUP), 0)
    c2 = lax.broadcasted_iota(jnp.int32, (2 * GROUP, GROUP), 1)
    averager = jnp.where(lax.rem(r2, GROUP) // HEAD == c2 // HEAD, 1.0 / HEAD, 0.0).astype(BF16)
    for g, lanes in enumerate(all_lanes):
        carried = (rkvg[0, :, lanes].astype(F32) * decays(levels, lanes) * valid).astype(BF16)
        held = state[:, lanes].astype(BF16)
        held = jnp.concatenate([held * m for m in ones_of], axis=0)
        wkv = local[g] + dot(carried, held, NT)
        big = wkv.astype(BF16)
        small = (wkv - big.astype(F32)).astype(BF16)
        centred = wkv - dot(jnp.concatenate([big, small], axis=1), averager)
        spread = dot((centred * centred).astype(BF16), averager[:GROUP])
        grouped = centred * lax.rsqrt(spread + 6.4e-4) * head_gain[:, lanes] + head_bias[:, lanes]
        gated[:, lanes] = (grouped * rkvg[3, :, lanes].astype(F32)).astype(BF16)


    ready(17)

    def partial(block):
        return dot(gated[...], emitted[:, pl.ds(pl.multiple_of(block * width, width), width)])

    index = 9 + len(doublings)
    give_far[...] = partial(corner).astype(BF16)
    first_give = remote(give_far, got_far, index, (s, mate))
    first_give.start()
    for_across = partial(across)
    first_give.wait_recv()
    give_sum[...] = (for_across + got_far[...].astype(F32)).astype(BF16)
    sum_give = remote(give_sum, got_sum, index + 1, (s, across))
    sum_give.start()
    give_near[...] = partial(mate).astype(BF16)
    second_give = remote(give_near, got_near, index + 2, (s, mate))
    second_give.start()
    total = xall[t].astype(F32) + partial(t)
    second_give.wait_recv()
    total = total + got_near[...].astype(F32)
    sum_give.wait_recv()
    out[...] = (total + got_sum[...].astype(F32)).astype(BF16)

    for copy in [over, side, *edges, pass_on, to_near, to_far, *sent]:
        copy.wait_send()
    for copy in [first_give, sum_give, second_give]:
        copy.wait_send()


def body(n, x, sizes, gain, bias, mixers, pile, left, right, fading, boost, head_gain, head_bias, emitted):
    rows, width = x.shape
    features, rank = left.shape
    doublings = max(1, (n // 2).bit_length() - 2)
    copies = 9 + doublings + 3
    spans = span_matrix(rows)
    vmem, hbm = pl.BlockSpec(memory_space=pltpu.VMEM), pl.BlockSpec(memory_space=pltpu.HBM)
    message = pltpu.VMEM((HEAD + 16, width), BF16)
    messages = pltpu.VMEM((doublings, HEAD + 16, width), BF16)
    block = pltpu.VMEM((rows, width), BF16)
    whole, part = pltpu.VMEM((1, features), F32), pltpu.VMEM((1, width), F32)
    return pl.pallas_call(
        functools.partial(kernel, n),
        out_shape=jax.ShapeDtypeStruct((rows, width), BF16),
        in_specs=[hbm] * 14,
        out_specs=vmem,
        scratch_shapes=[
            pltpu.SMEM(sizes.shape, jnp.int32),
            whole, whole, pltpu.VMEM(mixers.shape, F32), part, part, part, part,
            pltpu.VMEM((4, rows, width), BF16),
            pltpu.VMEM((4, EDGE, width), BF16),
            pltpu.VMEM(spans.shape, BF16),
            pltpu.VMEM((rank, features), BF16),
            pltpu.VMEM((rank, width), BF16),
            pltpu.VMEM(pile.shape, BF16),
            pltpu.VMEM(emitted.shape, BF16),
            pltpu.VMEM((5, rows, features), BF16),
            pltpu.VMEM((4, rows, width), BF16),
            block,
            message, message, message, messages, messages,
            block, block, block, block, block, block,
            pltpu.SemaphoreType.DMA((17,)),
            pltpu.SemaphoreType.DMA((copies,)),
            pltpu.SemaphoreType.DMA((copies,)),
        ],
        compiler_params=pltpu.CompilerParams(
            collective_id=0, has_side_effects=True, vmem_limit_bytes=63 * 1024 * 1024
        ),
    )(
        sizes, x, gain[None], bias[None], mixers, fading[None], boost[None],
        head_gain[None], head_bias[None], jnp.asarray(spans), left.T, right, pile, emitted,
    )


def solution(mesh):
    in_specs = (
        P("seq", "tp"), P(), P(), P(), P(), P(None, None, "tp"), P(), P(None, "tp"),
        P("tp"), P("tp"), P("tp"), P("tp"), P("tp", None),
    )
    return jax.shard_map(
        functools.partial(body, mesh.shape["seq"]),
        mesh=mesh, in_specs=in_specs, out_specs=P("seq", "tp"), check_vma=False,
    )
```

```python
import functools

import jax
import jax.numpy as jnp
import numpy as np
from jax import lax
from jax.experimental import pallas as pl
from jax.experimental.pallas import tpu as pltpu
from jax.sharding import PartitionSpec as P

HEAD = 64
GROUP = 256
EDGE = 16
BF16, F32 = jnp.bfloat16, jnp.float32
NT = (((1,), (1,)), ((), ()))
TN = (((0,), (0,)), ((), ()))


def span_matrix(rows):
    t, j = np.arange(rows)[:, None], np.arange(rows)[None, :]
    parts = []
    for level in range(rows.bit_length() - 1):
        same = (t >> level) == (j >> level)
        odd = ((t >> level) & 1) == 1
        parts.append(same & np.where(odd, j < t, j > t))
    parts += [j < t, j > t, np.ones((16, rows), bool)]
    spans = np.concatenate(parts, 0)
    return np.concatenate([spans, spans], 1).astype(jnp.bfloat16)


def dot(a, b, dims=None):
    if dims is None:
        return jnp.dot(a, b, preferred_element_type=F32)
    return lax.dot_general(a, b, dims, preferred_element_type=F32)


def kernel(
    n, sizes_h, x, gain_h, bias_h, mixers_h, fading_h, boost_h, head_gain_h, head_bias_h,
    spans_h, left_h, right_h, pile_h, emitted_h, out,
    sizes, gain, bias, mixers, fading, boost, head_gain, head_bias, xall, edge, spans, left, right, pile, emitted, mixed, rkvg, gated,
    mine, near, far, wide, came, give_far, got_far, give_near, got_near, give_sum, got_sum,
    load_sem, send_sem, recv_sem,
):
    rows, width = x.shape
    levels = rows.bit_length() - 1
    features = 4 * width
    groups = width // GROUP
    per_group = GROUP // HEAD
    s, t = lax.axis_index("seq"), lax.axis_index("tp")
    mate = t + 1 - 2 * lax.rem(t, 2)
    across = t + 2 - 4 * lax.div(t, 2)
    corner = 3 - t

    def ahead(d):
        return lax.rem(s + d, n)

    def behind(d):
        return lax.rem(s + n - d, n)

    def quarters(index):
        step = pile.shape[1] // 4
        cut = [pl.ds(i * step, step) for i in range(4)]
        return [(pile_h.at[index, part], pile.at[index, part]) for part in cut]

    wanted = [
        [(x, xall.at[t])], [(sizes_h, sizes)],
        [(gain_h, gain)], [(bias_h, bias)], [(mixers_h, mixers)],
        [(left_h, left)], [(right_h, right)], [(fading_h, fading)], [(spans_h, spans)],
        quarters(1), quarters(2), quarters(0),
        [(boost_h, boost)], quarters(3), [(head_gain_h, head_gain)],
        [(head_bias_h, head_bias)], [(emitted_h, emitted)],
    ]
    loads, used = [], 0
    for entry in wanted:
        loads.append([
            pltpu.make_async_copy(a, b, load_sem.at[used + i]) for i, (a, b) in enumerate(entry)
        ])
        used += len(entry)

    def begin_loads(first, end):
        for entry in loads[first:end]:
            for load in entry:
                load.start()

    unread = list(loads)

    def ready(upto):
        while len(loads) - len(unread) < upto:
            for load in unread.pop(0):
                load.wait()

    begin_loads(0, 11)

    hops = [1, 2]
    while hops[-1] * 2 < n // 2:
        hops.append(hops[-1] * 2)
    doublings = [d for d in hops if 2 <= d < n // 2]

    barrier = pltpu.get_barrier_semaphore()
    sources = [(s, mate), (s, across)] + [(behind(1), jnp.int32(j)) for j in range(4)]
    sources += [(behind(d), t) for d in hops[1:]]
    for source in sources:
        pl.semaphore_signal(barrier, inc=1, device_id=source, device_id_type=pl.DeviceIdType.MESH)
    pl.semaphore_wait(barrier, len(sources))

    def remote(src, dst, index, device):
        return pltpu.make_async_remote_copy(
            src_ref=src, dst_ref=dst, send_sem=send_sem.at[index], recv_sem=recv_sem.at[index],
            device_id=device, device_id_type=pl.DeviceIdType.MESH,
        )

    over = remote(x, xall.at[t], 0, (s, across))
    over.start()
    side = remote(x, xall.at[t], 1, (s, mate))
    side.start()
    tail_rows = x.at[pl.ds(rows - EDGE, EDGE)]
    edges = [
        remote(tail_rows, edge.at[t], 2 + j, (ahead(1), lax.rem(t + j, 4))) for j in range(4)
    ]
    for copy in edges:
        copy.start()
    ready(2)

    firsts = [jnp.int32(0)]
    for i in range(sizes.shape[0] - 1):
        firsts.append(firsts[-1] + sizes[i])

    def prompt_of(position):
        count = jnp.where(firsts[0] <= position, 1, 0)
        for first in firsts[1:]:
            count = count + jnp.where(first <= position, 1, 0)
        return count

    begin = s * rows
    order = lax.broadcasted_iota(jnp.int32, (rows, 1), 0)
    starts = begin + order == firsts[0]
    for first in firsts[1:]:
        starts = starts | (begin + order == first)
    going = jnp.where(starts, 0.0, 1.0)
    prompt = prompt_of(begin + order)
    entering, last = prompt_of(begin - 1), prompt_of(begin + rows - 1)
    valid = jnp.where(prompt == entering, 1.0, 0.0)
    tail_ok = jnp.where(prompt == last, 1.0, 0.0)
    keep = jnp.where(last == entering, 1.0, 0.0)

    over.wait_recv()
    begin_loads(11, len(loads))
    pass_on = remote(xall.at[across], xall.at[across], 6, (s, mate))
    pass_on.start()
    side.wait_recv()
    for copy in edges:
        copy.wait_recv()
    pass_on.wait_recv()


    ready(5)

    def moments(ref):
        total = sum(jnp.sum(ref[c].astype(F32), axis=1, keepdims=True) for c in range(4))
        mean = total / features
        square = 0.0
        for c in range(4):
            centred = ref[c].astype(F32) - mean
            square = square + jnp.sum(centred * centred, axis=1, keepdims=True)
        return mean, lax.rsqrt(square / features + 1e-5)

    mean, scale = moments(xall)
    edge_mean, edge_scale = moments(edge)
    for c in range(4):
        cols = slice(c * width, (c + 1) * width)
        base = ((xall[c].astype(F32) - mean) * scale * gain[:, cols] + bias[:, cols])
        base = base.astype(BF16).astype(F32)
        end = ((edge[c].astype(F32) - edge_mean) * edge_scale * gain[:, cols] + bias[:, cols])
        end = end.astype(BF16).astype(F32)
        previous = jnp.where(order == 0, end[EDGE - 1 :, :], pltpu.roll(base, 1, 0)) * going
        delta = previous - base
        for i in range(5):
            mixed[i, :, cols] = (base + delta * mixers[i : i + 1, cols]).astype(BF16)


    ready(9)
    lora = jnp.tanh(dot(mixed[4], left[...], NT)).astype(BF16)
    log_decay = -fading[...] * jnp.exp(dot(lora, right[...]))
    high = log_decay.astype(BF16)
    low = (log_decay - high.astype(F32)).astype(BF16)
    pair = jnp.concatenate([high, low], axis=0)

    def decays(block, lanes, count=rows):
        return jnp.exp(dot(spans[pl.ds(block * rows, count)], pair[:, lanes]))


    ready(10)
    rkvg[1] = dot(mixed[1], pile[1]).astype(BF16)
    ready(11)
    rkvg[2] = dot(mixed[2], pile[2]).astype(BF16)


    lane = lax.broadcasted_iota(jnp.int32, (1, GROUP), 1)
    of_head = [lane // HEAD == h for h in range(per_group)]
    ones_of = [jnp.where(m, 1.0, 0.0).astype(BF16) for m in of_head]
    all_lanes = [slice(g * GROUP, (g + 1) * GROUP) for g in range(groups)]
    for lanes in all_lanes:
        tail = (rkvg[1, :, lanes].astype(F32) * decays(levels + 1, lanes) * tail_ok).astype(BF16)
        full = dot(rkvg[2, :, lanes], tail, TN)
        state = jnp.where(of_head[0], full[:HEAD], 0.0)
        for h in range(1, per_group):
            state = state + jnp.where(of_head[h], full[h * HEAD : (h + 1) * HEAD], 0.0)
        mine[:HEAD, lanes] = state.astype(BF16)
        mine[HEAD:, lanes] = (decays(levels + 2, lanes, 16) * keep).astype(BF16)
    to_near = remote(mine, near, 7, (ahead(1), t))
    to_near.start()
    to_far = remote(mine, far, 8, (ahead(2), t))
    to_far.start()


    ready(13)
    rkvg[0] = dot(mixed[0], pile[0]).astype(BF16)


    row = lax.broadcasted_iota(jnp.int32, (rows, rows), 0)
    col = lax.broadcasted_iota(jnp.int32, (rows, rows), 1)
    together = prompt_of(begin + row) == prompt_of(begin + col)

    def pair_mask(level):
        if level == levels:
            return jnp.where(row == col, 1.0, 0.0)
        ok = (row >> (level + 1)) == (col >> (level + 1))
        ok = ok & (((row >> level) & 1) == 1) & (((col >> level) & 1) == 0)
        return jnp.where(ok & together, 1.0, 0.0)

    def local_part(lanes):
        recept, key, value = rkvg[0, :, lanes], rkvg[1, :, lanes], rkvg[2, :, lanes]
        scores = [0.0] * per_group
        for level in range(levels + 1):
            if level < levels:
                weight = decays(level, lanes).astype(BF16)
                asks, keys = recept * weight, key * weight
            else:
                asks, keys = (recept.astype(F32) * boost[:, lanes]).astype(BF16), key
            asks = jnp.concatenate([asks * m for m in ones_of], axis=0)
            found = dot(asks, keys, NT)
            mask = pair_mask(level)
            scores = [
                scores[h] + found[h * rows : (h + 1) * rows] * mask for h in range(per_group)
            ]
        scores = jnp.concatenate([p.astype(BF16) for p in scores], axis=1)
        values = jnp.concatenate([value * m for m in ones_of], axis=0)
        return dot(scores, values)

    local = [local_part(all_lanes[0])]


    to_near.wait_recv()
    to_far.wait_recv()

    reach = near[HEAD:].astype(F32)[:1]
    state = near[:HEAD].astype(F32) + reach * far[:HEAD].astype(F32)
    reach = reach * far[HEAD:].astype(F32)[:1]
    sent = []
    for i, d in enumerate(doublings):
        wide[i, :HEAD] = state.astype(BF16)
        wide[i, HEAD:] = jnp.broadcast_to(reach, (16, width)).astype(BF16)
        copy = remote(wide.at[i], came.at[i], 9 + i, (ahead(d), t))
        copy.start()
        sent.append(copy)
        if i == 0:
            local += [local_part(lanes) for lanes in all_lanes[1:]]
            ready(14)
            gate = dot(mixed[3], pile[3])
            rkvg[3] = (gate / (1.0 + jnp.exp(-gate))).astype(BF16)
        copy.wait_recv()
        state = state + reach * came[i, :HEAD].astype(F32)
        reach = reach * came[i, HEAD:].astype(F32)[:1]


    ready(16)
    r2 = lax.broadcasted_iota(jnp.int32, (2 * GROUP, GROUP), 0)
    c2 = lax.broadcasted_iota(jnp.int32, (2 * GROUP, GROUP), 1)
    averager = jnp.where(lax.rem(r2, GROUP) // HEAD == c2 // HEAD, 1.0 / HEAD, 0.0).astype(BF16)
    for g, lanes in enumerate(all_lanes):
        carried = (rkvg[0, :, lanes].astype(F32) * decays(levels, lanes) * valid).astype(BF16)
        held = state[:, lanes].astype(BF16)
        held = jnp.concatenate([held * m for m in ones_of], axis=0)
        wkv = local[g] + dot(carried, held, NT)
        big = wkv.astype(BF16)
        small = (wkv - big.astype(F32)).astype(BF16)
        centred = wkv - dot(jnp.concatenate([big, small], axis=1), averager)
        spread = dot((centred * centred).astype(BF16), averager[:GROUP])
        grouped = centred * lax.rsqrt(spread + 6.4e-4) * head_gain[:, lanes] + head_bias[:, lanes]
        gated[:, lanes] = (grouped * rkvg[3, :, lanes].astype(F32)).astype(BF16)


    ready(17)

    def partial(block):
        return dot(gated[...], emitted[:, pl.ds(pl.multiple_of(block * width, width), width)])

    index = 9 + len(doublings)
    give_far[...] = partial(corner).astype(BF16)
    first_give = remote(give_far, got_far, index, (s, mate))
    first_give.start()
    for_across = partial(across)
    first_give.wait_recv()
    give_sum[...] = (for_across + got_far[...].astype(F32)).astype(BF16)
    sum_give = remote(give_sum, got_sum, index + 1, (s, across))
    sum_give.start()
    give_near[...] = partial(mate).astype(BF16)
    second_give = remote(give_near, got_near, index + 2, (s, mate))
    second_give.start()
    total = xall[t].astype(F32) + partial(t)
    second_give.wait_recv()
    total = total + got_near[...].astype(F32)
    sum_give.wait_recv()
    out[...] = (total + got_sum[...].astype(F32)).astype(BF16)

    for copy in [over, side, *edges, pass_on, to_near, to_far, *sent]:
        copy.wait_send()
    for copy in [first_give, sum_give, second_give]:
        copy.wait_send()


def body(n, x, sizes, gain, bias, mixers, pile, left, right, fading, boost, head_gain, head_bias, emitted):
    rows, width = x.shape
    features, rank = left.shape
    doublings = max(1, (n // 2).bit_length() - 2)
    copies = 9 + doublings + 3
    spans = span_matrix(rows)
    vmem, hbm = pl.BlockSpec(memory_space=pltpu.VMEM), pl.BlockSpec(memory_space=pltpu.HBM)
    message = pltpu.VMEM((HEAD + 16, width), BF16)
    messages = pltpu.VMEM((doublings, HEAD + 16, width), BF16)
    block = pltpu.VMEM((rows, width), BF16)
    whole, part = pltpu.VMEM((1, features), F32), pltpu.VMEM((1, width), F32)
    return pl.pallas_call(
        functools.partial(kernel, n),
        out_shape=jax.ShapeDtypeStruct((rows, width), BF16),
        in_specs=[hbm] * 14,
        out_specs=vmem,
        scratch_shapes=[
            pltpu.SMEM(sizes.shape, jnp.int32),
            whole, whole, pltpu.VMEM(mixers.shape, F32), part, part, part, part,
            pltpu.VMEM((4, rows, width), BF16),
            pltpu.VMEM((4, EDGE, width), BF16),
            pltpu.VMEM(spans.shape, BF16),
            pltpu.VMEM((rank, features), BF16),
            pltpu.VMEM((rank, width), BF16),
            pltpu.VMEM(pile.shape, BF16),
            pltpu.VMEM(emitted.shape, BF16),
            pltpu.VMEM((5, rows, features), BF16),
            pltpu.VMEM((4, rows, width), BF16),
            block,
            message, message, message, messages, messages,
            block, block, block, block, block, block,
            pltpu.SemaphoreType.DMA((29,)),
            pltpu.SemaphoreType.DMA((copies,)),
            pltpu.SemaphoreType.DMA((copies,)),
        ],
        compiler_params=pltpu.CompilerParams(
            collective_id=0, has_side_effects=True, vmem_limit_bytes=63 * 1024 * 1024
        ),
    )(
        sizes, x, gain[None], bias[None], mixers, fading[None], boost[None],
        head_gain[None], head_bias[None], jnp.asarray(spans), left.T, right, pile, emitted,
    )


def solution(mesh):
    in_specs = (
        P("seq", "tp"), P(), P(), P(), P(), P(None, None, "tp"), P(), P(None, "tp"),
        P("tp"), P("tp"), P("tp"), P("tp"), P("tp", None),
    )
    return jax.shard_map(
        functools.partial(body, mesh.shape["seq"]),
        mesh=mesh, in_specs=in_specs, out_specs=P("seq", "tp"), check_vma=False,
    )
```

```python
import functools

import jax
import jax.numpy as jnp
import numpy as np
from jax import lax
from jax.experimental import pallas as pl
from jax.experimental.pallas import tpu as pltpu
from jax.sharding import PartitionSpec as P

HEAD = 64
GROUP = 256
EDGE = 16
BF16, F32 = jnp.bfloat16, jnp.float32
NT = (((1,), (1,)), ((), ()))
TN = (((0,), (0,)), ((), ()))


def span_matrix(rows):
    t, j = np.arange(rows)[:, None], np.arange(rows)[None, :]
    parts = []
    for level in range(rows.bit_length() - 1):
        same = (t >> level) == (j >> level)
        odd = ((t >> level) & 1) == 1
        parts.append(same & np.where(odd, j < t, j > t))
    parts += [j < t, j > t, np.ones((16, rows), bool)]
    spans = np.concatenate(parts, 0)
    return np.concatenate([spans, spans], 1).astype(jnp.bfloat16)


def dot(a, b, dims=None):
    if dims is None:
        return jnp.dot(a, b, preferred_element_type=F32)
    return lax.dot_general(a, b, dims, preferred_element_type=F32)


def kernel(
    n, sizes_h, x, gain_h, bias_h, mixers_h, fading_h, boost_h, head_gain_h, head_bias_h,
    spans_h, left_h, right_h, pile_h, emitted_h, out,
    sizes, gain, bias, mixers, fading, boost, head_gain, head_bias, xall, edge, spans, left, right, pile, emitted, mixed, rkvg, gated,
    mine, near, far, wide, came, give_far, got_far, give_near, got_near, give_sum, got_sum,
    load_sem, send_sem, recv_sem,
):
    rows, width = x.shape
    levels = rows.bit_length() - 1
    features = 4 * width
    groups = width // GROUP
    per_group = GROUP // HEAD
    s, t = lax.axis_index("seq"), lax.axis_index("tp")
    mate = t + 1 - 2 * lax.rem(t, 2)
    across = t + 2 - 4 * lax.div(t, 2)
    corner = 3 - t

    def ahead(d):
        return lax.rem(s + d, n)

    def behind(d):
        return lax.rem(s + n - d, n)

    wanted = [
        (x, xall.at[t]), (sizes_h, sizes), (gain_h, gain), (bias_h, bias), (mixers_h, mixers),
        (left_h, left), (right_h, right), (fading_h, fading), (spans_h, spans),
        (pile_h.at[1], pile.at[1]), (pile_h.at[2], pile.at[2]), (pile_h.at[0], pile.at[0]),
        (boost_h, boost), (pile_h.at[3], pile.at[3]), (head_gain_h, head_gain),
        (head_bias_h, head_bias), (emitted_h, emitted),
    ]
    loads = [pltpu.make_async_copy(a, b, load_sem.at[i]) for i, (a, b) in enumerate(wanted)]
    for load in loads:
        load.start()
    unread = list(loads)

    def ready(upto):
        while len(loads) - len(unread) < upto:
            unread.pop(0).wait()

    hops = [1, 2]
    while hops[-1] * 2 < n // 2:
        hops.append(hops[-1] * 2)
    doublings = [d for d in hops if 2 <= d < n // 2]

    barrier = pltpu.get_barrier_semaphore()
    sources = [(s, mate), (s, across)] + [(behind(1), jnp.int32(j)) for j in range(4)]
    sources += [(behind(d), t) for d in hops[1:]]
    for source in sources:
        pl.semaphore_signal(barrier, inc=1, device_id=source, device_id_type=pl.DeviceIdType.MESH)
    pl.semaphore_wait(barrier, len(sources))

    def remote(src, dst, index, device):
        return pltpu.make_async_remote_copy(
            src_ref=src, dst_ref=dst, send_sem=send_sem.at[index], recv_sem=recv_sem.at[index],
            device_id=device, device_id_type=pl.DeviceIdType.MESH,
        )

    over = remote(x, xall.at[t], 0, (s, across))
    over.start()
    side = remote(x, xall.at[t], 1, (s, mate))
    side.start()
    tail_rows = x.at[pl.ds(rows - EDGE, EDGE)]
    edges = [
        remote(tail_rows, edge.at[t], 2 + j, (ahead(1), lax.rem(t + j, 4))) for j in range(4)
    ]
    for copy in edges:
        copy.start()
    ready(2)

    firsts = [jnp.int32(0)]
    for i in range(sizes.shape[0] - 1):
        firsts.append(firsts[-1] + sizes[i])

    def prompt_of(position):
        count = jnp.where(firsts[0] <= position, 1, 0)
        for first in firsts[1:]:
            count = count + jnp.where(first <= position, 1, 0)
        return count

    begin = s * rows
    order = lax.broadcasted_iota(jnp.int32, (rows, 1), 0)
    starts = begin + order == firsts[0]
    for first in firsts[1:]:
        starts = starts | (begin + order == first)
    going = jnp.where(starts, 0.0, 1.0)
    prompt = prompt_of(begin + order)
    entering, last = prompt_of(begin - 1), prompt_of(begin + rows - 1)
    valid = jnp.where(prompt == entering, 1.0, 0.0)
    tail_ok = jnp.where(prompt == last, 1.0, 0.0)
    keep = jnp.where(last == entering, 1.0, 0.0)

    over.wait_recv()
    pass_on = remote(xall.at[across], xall.at[across], 6, (s, mate))
    pass_on.start()
    side.wait_recv()
    for copy in edges:
        copy.wait_recv()
    pass_on.wait_recv()


    ready(5)

    def moments(ref):
        total = sum(jnp.sum(ref[c].astype(F32), axis=1, keepdims=True) for c in range(4))
        mean = total / features
        square = 0.0
        for c in range(4):
            centred = ref[c].astype(F32) - mean
            square = square + jnp.sum(centred * centred, axis=1, keepdims=True)
        return mean, lax.rsqrt(square / features + 1e-5)

    mean, scale = moments(xall)
    edge_mean, edge_scale = moments(edge)
    for c in range(4):
        cols = slice(c * width, (c + 1) * width)
        base = ((xall[c].astype(F32) - mean) * scale * gain[:, cols] + bias[:, cols])
        base = base.astype(BF16).astype(F32)
        end = ((edge[c].astype(F32) - edge_mean) * edge_scale * gain[:, cols] + bias[:, cols])
        end = end.astype(BF16).astype(F32)
        previous = jnp.where(order == 0, end[EDGE - 1 :, :], pltpu.roll(base, 1, 0)) * going
        delta = previous - base
        for i in range(5):
            mixed[i, :, cols] = (base + delta * mixers[i : i + 1, cols]).astype(BF16)


    ready(9)
    lora = jnp.tanh(dot(mixed[4], left[...], NT)).astype(BF16)
    log_decay = -fading[...] * jnp.exp(dot(lora, right[...]))
    high = log_decay.astype(BF16)
    low = (log_decay - high.astype(F32)).astype(BF16)
    pair = jnp.concatenate([high, low], axis=0)

    def decays(block, lanes, count=rows):
        return jnp.exp(dot(spans[pl.ds(block * rows, count)], pair[:, lanes]))


    ready(10)
    rkvg[1] = dot(mixed[1], pile[1]).astype(BF16)
    ready(11)
    rkvg[2] = dot(mixed[2], pile[2]).astype(BF16)


    lane = lax.broadcasted_iota(jnp.int32, (1, GROUP), 1)
    of_head = [lane // HEAD == h for h in range(per_group)]
    ones_of = [jnp.where(m, 1.0, 0.0).astype(BF16) for m in of_head]
    all_lanes = [slice(g * GROUP, (g + 1) * GROUP) for g in range(groups)]
    to_near, to_far = [], []
    for g, lanes in enumerate(all_lanes):
        tail = (rkvg[1, :, lanes].astype(F32) * decays(levels + 1, lanes) * tail_ok).astype(BF16)
        full = dot(rkvg[2, :, lanes], tail, TN)
        state = jnp.where(of_head[0], full[:HEAD], 0.0)
        for h in range(1, per_group):
            state = state + jnp.where(of_head[h], full[h * HEAD : (h + 1) * HEAD], 0.0)
        mine[g, :HEAD] = state.astype(BF16)
        mine[g, HEAD:] = (decays(levels + 2, lanes, 16) * keep).astype(BF16)
        to_near.append(remote(mine.at[g], near.at[g], 7 + g, (ahead(1), t)))
        to_near[g].start()
        to_far.append(remote(mine.at[g], far.at[g], 7 + groups + g, (ahead(2), t)))
        to_far[g].start()

    ready(13)
    rkvg[0] = dot(mixed[0], pile[0]).astype(BF16)


    row = lax.broadcasted_iota(jnp.int32, (rows, rows), 0)
    col = lax.broadcasted_iota(jnp.int32, (rows, rows), 1)
    together = prompt_of(begin + row) == prompt_of(begin + col)

    def pair_mask(level):
        if level == levels:
            return jnp.where(row == col, 1.0, 0.0)
        ok = (row >> (level + 1)) == (col >> (level + 1))
        ok = ok & (((row >> level) & 1) == 1) & (((col >> level) & 1) == 0)
        return jnp.where(ok & together, 1.0, 0.0)

    def local_part(lanes):
        recept, key, value = rkvg[0, :, lanes], rkvg[1, :, lanes], rkvg[2, :, lanes]
        scores = [0.0] * per_group
        for level in range(levels + 1):
            if level < levels:
                weight = decays(level, lanes).astype(BF16)
                asks, keys = recept * weight, key * weight
            else:
                asks, keys = (recept.astype(F32) * boost[:, lanes]).astype(BF16), key
            asks = jnp.concatenate([asks * m for m in ones_of], axis=0)
            found = dot(asks, keys, NT)
            mask = pair_mask(level)
            scores = [
                scores[h] + found[h * rows : (h + 1) * rows] * mask for h in range(per_group)
            ]
        scores = jnp.concatenate([p.astype(BF16) for p in scores], axis=1)
        values = jnp.concatenate([value * m for m in ones_of], axis=0)
        return dot(scores, values)

    local = [local_part(all_lanes[0])]


    base_index = 7 + 2 * groups
    state, reach, sent = [None] * groups, [None] * groups, []

    def fold(i, g):
        sent[i * groups + g].wait_recv()
        state[g] = state[g] + reach[g] * came[i, g, :HEAD].astype(F32)
        reach[g] = reach[g] * came[i, g, HEAD:].astype(F32)[:1]

    for i, d in enumerate(doublings):
        for g in range(groups):
            if i == 0:
                to_near[g].wait_recv()
                to_far[g].wait_recv()
                by_near = near[g, HEAD:].astype(F32)[:1]
                state[g] = near[g, :HEAD].astype(F32) + by_near * far[g, :HEAD].astype(F32)
                reach[g] = by_near * far[g, HEAD:].astype(F32)[:1]
            else:
                fold(i - 1, g)
            wide[i, g, :HEAD] = state[g].astype(BF16)
            wide[i, g, HEAD:] = jnp.broadcast_to(reach[g], (16, GROUP)).astype(BF16)
            place = base_index + i * groups + g
            sent.append(remote(wide.at[i, g], came.at[i, g], place, (ahead(d), t)))
            sent[-1].start()
        if i == 0:
            local += [local_part(lanes) for lanes in all_lanes[1:]]
            ready(14)
            gate = dot(mixed[3], pile[3])
            rkvg[3] = (gate / (1.0 + jnp.exp(-gate))).astype(BF16)

    ready(16)
    r2 = lax.broadcasted_iota(jnp.int32, (2 * GROUP, GROUP), 0)
    c2 = lax.broadcasted_iota(jnp.int32, (2 * GROUP, GROUP), 1)
    averager = jnp.where(lax.rem(r2, GROUP) // HEAD == c2 // HEAD, 1.0 / HEAD, 0.0).astype(BF16)
    for g, lanes in enumerate(all_lanes):
        fold(len(doublings) - 1, g)
        carried = (rkvg[0, :, lanes].astype(F32) * decays(levels, lanes) * valid).astype(BF16)
        held = state[g].astype(BF16)
        held = jnp.concatenate([held * m for m in ones_of], axis=0)
        wkv = local[g] + dot(carried, held, NT)
        big = wkv.astype(BF16)
        small = (wkv - big.astype(F32)).astype(BF16)
        centred = wkv - dot(jnp.concatenate([big, small], axis=1), averager)
        spread = dot((centred * centred).astype(BF16), averager[:GROUP])
        grouped = centred * lax.rsqrt(spread + 6.4e-4) * head_gain[:, lanes] + head_bias[:, lanes]
        gated[:, lanes] = (grouped * rkvg[3, :, lanes].astype(F32)).astype(BF16)


    ready(17)

    def partial(block):
        return dot(gated[...], emitted[:, pl.ds(pl.multiple_of(block * width, width), width)])

    index = base_index + groups * len(doublings)
    give_far[...] = partial(corner).astype(BF16)
    first_give = remote(give_far, got_far, index, (s, mate))
    first_give.start()
    for_across = partial(across)
    first_give.wait_recv()
    give_sum[...] = (for_across + got_far[...].astype(F32)).astype(BF16)
    sum_give = remote(give_sum, got_sum, index + 1, (s, across))
    sum_give.start()
    give_near[...] = partial(mate).astype(BF16)
    second_give = remote(give_near, got_near, index + 2, (s, mate))
    second_give.start()
    total = xall[t].astype(F32) + partial(t)
    second_give.wait_recv()
    total = total + got_near[...].astype(F32)
    sum_give.wait_recv()
    out[...] = (total + got_sum[...].astype(F32)).astype(BF16)

    for copy in [over, side, *edges, pass_on, *to_near, *to_far, *sent]:
        copy.wait_send()
    for copy in [first_give, sum_give, second_give]:
        copy.wait_send()


def body(n, x, sizes, gain, bias, mixers, pile, left, right, fading, boost, head_gain, head_bias, emitted):
    rows, width = x.shape
    features, rank = left.shape
    doublings = max(1, (n // 2).bit_length() - 2)
    groups = width // GROUP
    copies = 7 + groups * (2 + doublings) + 3
    spans = span_matrix(rows)
    vmem, hbm = pl.BlockSpec(memory_space=pltpu.VMEM), pl.BlockSpec(memory_space=pltpu.HBM)
    message = pltpu.VMEM((groups, HEAD + 16, GROUP), BF16)
    messages = pltpu.VMEM((doublings, groups, HEAD + 16, GROUP), BF16)
    block = pltpu.VMEM((rows, width), BF16)
    whole, part = pltpu.VMEM((1, features), F32), pltpu.VMEM((1, width), F32)
    return pl.pallas_call(
        functools.partial(kernel, n),
        out_shape=jax.ShapeDtypeStruct((rows, width), BF16),
        in_specs=[hbm] * 14,
        out_specs=vmem,
        scratch_shapes=[
            pltpu.SMEM(sizes.shape, jnp.int32),
            whole, whole, pltpu.VMEM(mixers.shape, F32), part, part, part, part,
            pltpu.VMEM((4, rows, width), BF16),
            pltpu.VMEM((4, EDGE, width), BF16),
            pltpu.VMEM(spans.shape, BF16),
            pltpu.VMEM((rank, features), BF16),
            pltpu.VMEM((rank, width), BF16),
            pltpu.VMEM(pile.shape, BF16),
            pltpu.VMEM(emitted.shape, BF16),
            pltpu.VMEM((5, rows, features), BF16),
            pltpu.VMEM((4, rows, width), BF16),
            block,
            message, message, message, messages, messages,
            block, block, block, block, block, block,
            pltpu.SemaphoreType.DMA((17,)),
            pltpu.SemaphoreType.DMA((copies,)),
            pltpu.SemaphoreType.DMA((copies,)),
        ],
        compiler_params=pltpu.CompilerParams(
            collective_id=0, has_side_effects=True, vmem_limit_bytes=63 * 1024 * 1024
        ),
    )(
        sizes, x, gain[None], bias[None], mixers, fading[None], boost[None],
        head_gain[None], head_bias[None], jnp.asarray(spans), left.T, right, pile, emitted,
    )


def solution(mesh):
    in_specs = (
        P("seq", "tp"), P(), P(), P(), P(), P(None, None, "tp"), P(), P(None, "tp"),
        P("tp"), P("tp"), P("tp"), P("tp"), P("tp", None),
    )
    return jax.shard_map(
        functools.partial(body, mesh.shape["seq"]),
        mesh=mesh, in_specs=in_specs, out_specs=P("seq", "tp"), check_vma=False,
    )
```
